512 devices in a mesh: snap: 64 (over y, z_lo, core), space: 8 (over x, z_hi).
Axes of the slice: x: 4, y: 8, z: 8 (z_hi: 2, z_lo: 4; z = z_hi * 4 + z_lo), core: 2. Of those that a mesh axis runs over, the one named last changes fastest.
Arguments:
- snapshots: bfloat16 [8192, 12288], P('snap', 'space'), may hold values from -6 to 6
- counts: int32 [64], P('snap'), may hold values from 1 to 128, 6144 in all
- weights: float32 [12288], P('space'), may hold values from 0.2 to 5
Outputs:
- gram: float32 [64, 33, 128, 128], P('snap', None, 'space')
The draws below stay inside these ranges and needn't reach their ends.
Inputs may be any that keep to these rules, and one draw needn't show every extreme that they name: The counts of all blocks sum to 6144, and some block is full.
All inputs are finite; a program needn't handle non-finite values.
Results may differ from the reference program's by a relative error of at most 0.0016.
Values may be sent and summed in bfloat16 or wider, within the bound.
No kernel may reach another device: no remote copies, remote signals or barrier semaphores. Data moves between devices by JAX's collectives and lax.ppermute only.
A program may use at most 64 MiB of HBM per device.

```python
import math
import jax
import jax.numpy as jnp
import numpy as np
from jax import lax

CAP = 128
NBLK = 64
SNAPS = 8192
POINTS = 12288
SPAN = 33
N_SNAP = 64


def block_levels(stream_key, extent, pieces, low, top_value):
    gain, own = 1.0, jax.random.fold_in(stream_key, 6)
    for position, parts in pieces:
        steps = jnp.exp(jax.random.uniform(jax.random.fold_in(own, position), (parts,), jnp.float32, low / len(pieces), top_value / len(pieces)))
        gain = gain * jnp.repeat(steps, extent[position] // parts).reshape([-1 if axis == position else 1 for axis in range(len(extent))])
    return gain


def length_profile(count, total, limit, skew):
    weights = [(1 << 20) // math.isqrt(rank ** skew) + 1 for rank in range(2, count + 1)]
    spare, given = total - limit - (count - 1), [1] * (count - 1)
    while spare > 0:
        candidates = [i for i in range(count - 1) if given[i] < limit]
        mass, remaining = sum([weights[i] for i in candidates]), spare
        for i in candidates:
            extra = min(limit - given[i], max(1, remaining * weights[i] // mass), spare)
            given[i] = given[i] + extra
            spare = spare - extra
    return np.array([limit] + given)


def uneven_parts(stream_key, count, total, reach, slope):
    if count == 2:
        one = jax.random.randint(stream_key, (), max(1, total - reach), min(reach, total - 1) + 1)
        return jnp.stack([one, total - one])
    tallies = jnp.asarray(length_profile(count, total, reach, slope), jnp.int32)
    couples = (count - 1) // 2
    source_of, sink = tallies[1:1 + 2 * couples:2], tallies[2:2 + 2 * couples:2]
    margin = jnp.minimum(source_of - 1, reach - sink)
    moved = jax.random.randint(jax.random.fold_in(stream_key, 1), (couples,), 0, 1 << 20) % (margin + 1)
    tallies = tallies.at[1:1 + 2 * couples:2].set(source_of - moved).at[2:2 + 2 * couples:2].set(sink + moved)
    return tallies[jax.random.permutation(jax.random.fold_in(stream_key, 2), count)]


def centred(stream_key, shape, scale, bound, split=(), kind=jnp.bfloat16):
    drawn = scale * jax.random.normal(stream_key, shape, jnp.float32)
    if split:
        drawn = drawn * block_levels(stream_key, shape, split, -0.22, 0.18)
    return jnp.clip(drawn, -bound, bound).astype(kind)


def setup_inputs(seed: int = 0) -> dict:
    streams_of = jax.random.split(jax.random.key(seed), 4)
    snapshots = centred(streams_of[0], (SNAPS, POINTS), 1.0, 6.0, ((0, 64), (1, 8)))
    counts = uneven_parts(streams_of[1], NBLK, N_SNAP * CAP * 3 // 4, CAP, 2).astype(jnp.int32)
    weights = jnp.clip(jnp.exp(math.log(5.0) - 3.218876 * jax.random.uniform(streams_of[2], (POINTS,), jnp.float32) ** block_levels(streams_of[2], (POINTS,), ((0, 8),), -0.2, 0.2)), 0.2, 5.0)
    return {"snapshots": snapshots, "counts": counts, "weights": weights}


def reference(snapshots, counts, weights):
    blocks = snapshots.reshape(N_SNAP, CAP, POINTS)
    live_rows = (jnp.arange(CAP, dtype=jnp.int32)[None, :] < counts[:, None])[:, :, None]
    masked = jnp.where(live_rows, blocks, jnp.zeros_like(blocks))
    weighted = (masked.astype(jnp.float32) * weights[None, None, :]).astype(jnp.bfloat16)
    left_rows = weighted.astype(jnp.float32)
    right_rows = masked.astype(jnp.float32)
    factor = 1.0 / math.sqrt(POINTS)

    def offset_tiles(offset):
        rolled = jnp.roll(right_rows, -offset, axis=0)
        return jnp.einsum('bcp,bdp->bcd', left_rows, rolled, precision=lax.Precision.HIGHEST) * factor
    tile_set = lax.map(offset_tiles, jnp.arange(SPAN, dtype=jnp.int32))
    return jnp.transpose(tile_set, (1, 0, 2, 3))
```

```python
import functools
import math

import jax
import jax.numpy as jnp
from jax import lax
from jax.experimental import pallas as pl
from jax.experimental.pallas import tpu as pltpu
from jax.sharding import Mesh
from jax.sharding import PartitionSpec as P

SIZES = {"y": 8, "zl": 4, "core": 2, "x": 4, "zh": 2}
ROW = 8
FAR = 4
VMEM = pl.BlockSpec(memory_space=pltpu.VMEM)
SMEM = pl.BlockSpec(memory_space=pltpu.SMEM)
PARAMS = pltpu.CompilerParams(vmem_limit_bytes=24 * 1024 * 1024)


def ahead(block, by):
    return lax.ppermute(block, "y", [(i, (i - by) % SIZES["y"]) for i in range(SIZES["y"])])


def across(block, flip):
    return lax.ppermute(block, "zl", [(i, i ^ flip) for i in range(SIZES["zl"])])


def swapped(block):
    return lax.ppermute(block, "core", [(0, 1), (1, 0)])


def tiles_kernel(place_ref, *refs):
    lefts, rights, out_ref, all_rights = refs[:8], refs[8:13], refs[13], refs[14]
    rows = rights[0].shape[0]
    share = rows // SIZES["x"]
    zl, core = place_ref[0], place_ref[1]
    mine = zl * 2 + core
    for d in range(FAR + 1):
        all_rights[pl.ds(d * rows, rows), :] = rights[d][...]
    contract = (((1,), (1,)), ((), ()))
    for n in range(ROW):
        flip, other = n % 4, n // 4
        zl_n = jnp.bitwise_xor(zl, flip)
        core_n = jnp.bitwise_xor(core, other)
        target = zl_n * 2 + core_n
        first = jnp.where(target < mine, 0, 1)
        right = all_rights[pl.ds(pl.multiple_of(first * rows, rows), FAR * rows), :]
        tile = lax.dot_general(
            lefts[n][...], right, contract, preferred_element_type=jnp.float32
        ).astype(jnp.bfloat16)
        for t in range(FAR):
            for x in range(SIZES["x"]):
                out_ref[x, target * FAR + t] = tile[
                    x * share : (x + 1) * share, t * rows : (t + 1) * rows
                ]
    own = lax.dot_general(
        lefts[0][...], rights[0][...], contract, preferred_element_type=jnp.float32
    )
    high = own.astype(jnp.bfloat16)
    low = (own - high.astype(jnp.float32)).astype(jnp.bfloat16)
    for x in range(SIZES["x"]):
        out_ref[x, ROW * FAR] = high[x * share : (x + 1) * share]
        out_ref[x, ROW * FAR + 1] = low[x * share : (x + 1) * share]


def first_sum_kernel(place_ref, parts_ref, out_ref, keep_ref, give_ref):
    half = out_ref.shape[2]
    zh = place_ref[2]

    def total(tile):
        acc = parts_ref[0, tile].astype(jnp.float32)
        for x in range(1, SIZES["x"]):
            acc = acc + parts_ref[x, tile].astype(jnp.float32)
        return acc

    for target in range(ROW):
        for t in range(FAR):
            acc = total(target * FAR + t).astype(jnp.bfloat16)
            for h in range(SIZES["zh"]):
                out_ref[target * SIZES["zh"] + h, t] = acc[h * half : (h + 1) * half]
    own = total(ROW * FAR) + total(ROW * FAR + 1)
    upper, lower = own[:half], own[half:]
    keep_ref[...] = jnp.where(zh == 0, upper, lower)
    give_ref[...] = jnp.where(zh == 0, lower, upper)


def last_sum_kernel(factor, place_ref, parts_ref, keep_ref, got_ref, out_ref):
    mine = place_ref[0] * 2 + place_ref[1]
    out_ref[0, 0] = (keep_ref[...] + got_ref[...]) * factor
    for j in range(1, ROW + 1):
        source = lax.rem(mine + j, ROW)
        for t in range(FAR):
            a = parts_ref[source * 2, t].astype(jnp.float32)
            b = parts_ref[source * 2 + 1, t].astype(jnp.float32)
            out_ref[0, ROW * t + j] = (a + b) * factor


def on_device(snapshots, counts, weights):
    rows, points = snapshots.shape
    slot_index = lax.broadcasted_iota(jnp.int32, (rows, 1), 0)
    masked = jnp.where(slot_index < counts[0], snapshots, jnp.zeros_like(snapshots))
    weighted = (masked.astype(jnp.float32) * weights[None, :]).astype(jnp.bfloat16)
    place = jnp.stack(
        [lax.axis_index("zl"), lax.axis_index("core"), lax.axis_index("zh")]
    ).astype(jnp.int32)

    z2, z3 = across(weighted, 2), across(weighted, 3)
    r4, r1 = ahead(masked, 4), ahead(masked, 1)
    z1 = across(weighted, 1)
    r3, r2 = ahead(r4, -1), ahead(r1, 1)
    lefts = [weighted, z1, z2, z3]
    lefts = lefts + [swapped(b) for b in lefts]
    rights = [masked, r1, r2, r3, r4]

    share, half = rows // SIZES["x"], rows // (SIZES["x"] * SIZES["zh"])
    tiles = pl.pallas_call(
        tiles_kernel,
        out_shape=jax.ShapeDtypeStruct(
            (SIZES["x"], ROW * FAR + 2, share, rows), jnp.bfloat16
        ),
        in_specs=[SMEM] + [VMEM] * 13,
        out_specs=VMEM,
        scratch_shapes=[pltpu.VMEM(((FAR + 1) * rows, points), jnp.bfloat16)],
        compiler_params=PARAMS,
    )(place, *lefts, *rights)
    parts = lax.all_to_all(tiles, "x", 0, 0, tiled=True)
    sums, keep, give = pl.pallas_call(
        first_sum_kernel,
        out_shape=(
            jax.ShapeDtypeStruct((ROW * SIZES["zh"], FAR, half, rows), jnp.bfloat16),
            jax.ShapeDtypeStruct((half, rows), jnp.float32),
            jax.ShapeDtypeStruct((half, rows), jnp.float32),
        ),
        in_specs=[SMEM, VMEM],
        out_specs=(VMEM, VMEM, VMEM),
        compiler_params=PARAMS,
    )(place, parts)
    got = lax.ppermute(give, "zh", [(0, 1), (1, 0)])
    shares = lax.all_to_all(sums, ("zl", "core", "zh"), 0, 0, tiled=True)
    factor = 1.0 / math.sqrt(points * SIZES["x"] * SIZES["zh"])
    return pl.pallas_call(
        functools.partial(last_sum_kernel, factor),
        out_shape=jax.ShapeDtypeStruct((1, ROW * FAR + 1, half, rows), jnp.float32),
        in_specs=[SMEM, VMEM, VMEM, VMEM],
        out_specs=VMEM,
        compiler_params=PARAMS,
    )(place, shares, keep, got)


def solution(mesh):
    fine = Mesh(mesh.devices.reshape(tuple(SIZES.values())), tuple(SIZES))
    snap, space = ("y", "zl", "core"), ("x", "zh")
    return jax.shard_map(
        on_device,
        mesh=fine,
        in_specs=(P(snap, space), P(snap), P(space)),
        out_specs=P(snap, None, space, None),
        check_vma=False,
    )
```

```python
import functools
import math

import jax
import jax.numpy as jnp
from jax import lax
from jax.experimental import pallas as pl
from jax.experimental.pallas import tpu as pltpu
from jax.sharding import Mesh
from jax.sharding import PartitionSpec as P

SIZES = {"y": 8, "zl": 4, "core": 2, "x": 4, "zh": 2}
ROW = 8
FAR = 4
EACH = 8
VMEM = pl.BlockSpec(memory_space=pltpu.VMEM)
SMEM = pl.BlockSpec(memory_space=pltpu.SMEM)
PARAMS = pltpu.CompilerParams(vmem_limit_bytes=32 * 1024 * 1024)


def ahead(block, by):
    return lax.ppermute(block, "y", [(i, (i - by) % SIZES["y"]) for i in range(SIZES["y"])])


def across(block, flip):
    return lax.ppermute(block, "zl", [(i, i ^ flip) for i in range(SIZES["zl"])])


def swapped(block):
    return lax.ppermute(block, "core", [(0, 1), (1, 0)])


def product(left_rows, right_rows):
    return lax.dot_general(
        left_rows, right_rows, (((1,), (1,)), ((), ())), preferred_element_type=jnp.float32
    )


def tiles_kernel(place_ref, *refs):
    lefts, rights, out_ref, left_all, right_all, dots = refs[:4], refs[4:14], *refs[14:]
    rows = rights[0].shape[0]
    share = rows // SIZES["x"]
    zl, core = place_ref[0], place_ref[1]
    for n in range(4):
        left_all[n * rows : (n + 1) * rows] = lefts[n][...]
    for n in range(10):
        right_all[n * rows : (n + 1) * rows] = rights[n][...]
    dots[...] = product(left_all[...], right_all[...])
    for flip in range(4):
        target = jnp.bitwise_xor(zl, flip)
        for other in range(2):
            side = jnp.bitwise_xor(core, other)
            first = jnp.where(zl * 2 + side > target * 2 + core, 0, 1)
            for t in range(FAR):
                start = pl.multiple_of((other * (FAR + 1) + t + first) * rows, rows)
                tile = dots[flip * rows : (flip + 1) * rows, pl.ds(start, rows)]
                tile = tile.astype(jnp.bfloat16)
                for x in range(SIZES["x"]):
                    out_ref[x, target * EACH + side * FAR + t] = tile[
                        x * share : (x + 1) * share
                    ]


def first_sum_kernel(parts_ref, out_ref):
    half = out_ref.shape[2]
    for target in range(4):
        for n in range(EACH):
            acc = parts_ref[0, target * EACH + n].astype(jnp.float32)
            for x in range(1, SIZES["x"]):
                acc = acc + parts_ref[x, target * EACH + n].astype(jnp.float32)
            acc = acc.astype(jnp.bfloat16)
            for h in range(SIZES["zh"]):
                out_ref[target * SIZES["zh"] + h, n] = acc[h * half : (h + 1) * half]


def last_sum_kernel(factor, place_ref, parts_ref, own_ref, out_ref):
    mine = place_ref[0] * 2 + place_ref[1]
    out_ref[0, 0] = own_ref[...] * factor
    for j in range(1, ROW + 1):
        source = lax.rem(mine + j, ROW)
        zl, core = lax.div(source, 2), lax.rem(source, 2)
        for t in range(FAR):
            a = parts_ref[zl * 2, core * FAR + t].astype(jnp.float32)
            b = parts_ref[zl * 2 + 1, core * FAR + t].astype(jnp.float32)
            out_ref[0, ROW * t + j] = (a + b) * factor


def on_device(snapshots, counts, weights):
    rows, points = snapshots.shape
    slot_index = lax.broadcasted_iota(jnp.int32, (rows, 1), 0)
    masked = jnp.where(slot_index < counts[0], snapshots, jnp.zeros_like(snapshots))
    weighted = (masked.astype(jnp.float32) * weights[None, :]).astype(jnp.bfloat16)
    place = jnp.stack([lax.axis_index("zl"), lax.axis_index("core")]).astype(jnp.int32)

    z2, z3, z1 = across(weighted, 2), across(weighted, 3), across(weighted, 1)
    r4, r1 = ahead(masked, 4), ahead(masked, 1)
    r3, r2 = ahead(r4, -1), ahead(r1, 1)
    lefts = [weighted, z1, z2, z3]
    rights = [masked, r1, r2, r3, r4]
    rights = rights + [swapped(b) for b in rights]
    own = lax.psum_scatter(
        product(weighted, masked), ("x", "zh"), scatter_dimension=0, tiled=True
    )

    share, half = rows // SIZES["x"], rows // (SIZES["x"] * SIZES["zh"])
    tiles = pl.pallas_call(
        tiles_kernel,
        out_shape=jax.ShapeDtypeStruct((SIZES["x"], 4 * EACH, share, rows), jnp.bfloat16),
        in_specs=[SMEM] + [VMEM] * 14,
        out_specs=VMEM,
        scratch_shapes=[
            pltpu.VMEM((4 * rows, points), jnp.bfloat16),
            pltpu.VMEM((10 * rows, points), jnp.bfloat16),
            pltpu.VMEM((4 * rows, 10 * rows), jnp.float32),
        ],
        compiler_params=PARAMS,
    )(place, *lefts, *rights)
    parts = lax.all_to_all(tiles, "x", 0, 0, tiled=True)
    sums = pl.pallas_call(
        first_sum_kernel,
        out_shape=jax.ShapeDtypeStruct((4 * SIZES["zh"], EACH, half, rows), jnp.bfloat16),
        in_specs=[VMEM],
        out_specs=VMEM,
        compiler_params=PARAMS,
    )(parts)
    shares = lax.all_to_all(sums, ("zl", "zh"), 0, 0, tiled=True)
    factor = 1.0 / math.sqrt(points * SIZES["x"] * SIZES["zh"])
    return pl.pallas_call(
        functools.partial(last_sum_kernel, factor),
        out_shape=jax.ShapeDtypeStruct((1, ROW * FAR + 1, half, rows), jnp.float32),
        in_specs=[SMEM, VMEM, VMEM],
        out_specs=VMEM,
        compiler_params=PARAMS,
    )(place, shares, own)


def solution(mesh):
    fine = Mesh(mesh.devices.reshape(tuple(SIZES.values())), tuple(SIZES))
    snap, space = ("y", "zl", "core"), ("x", "zh")
    return jax.shard_map(
        on_device,
        mesh=fine,
        in_specs=(P(snap, space), P(snap), P(space)),
        out_specs=P(snap, None, space, None),
        check_vma=False,
    )
```

```python
import functools
import math

import jax
import jax.numpy as jnp
from jax import lax
from jax.experimental import pallas as pl
from jax.experimental.pallas import tpu as pltpu
from jax.sharding import Mesh
from jax.sharding import PartitionSpec as P

SIZES = {"y": 8, "zl": 4, "core": 2, "x": 4, "zh": 2}
ROW = 8
FAR = 4
EACH = 8
VMEM = pl.BlockSpec(memory_space=pltpu.VMEM)
SMEM = pl.BlockSpec(memory_space=pltpu.SMEM)
PARAMS = pltpu.CompilerParams(vmem_limit_bytes=32 * 1024 * 1024)


def ahead(block, by):
    return lax.ppermute(block, "y", [(i, (i - by) % SIZES["y"]) for i in range(SIZES["y"])])


def across(block, flip):
    return lax.ppermute(block, "zl", [(i, i ^ flip) for i in range(SIZES["zl"])])


def swapped(block):
    return lax.ppermute(block, "core", [(0, 1), (1, 0)])


def product(left_rows, right_rows):
    return lax.dot_general(
        left_rows, right_rows, (((1,), (1,)), ((), ())), preferred_element_type=jnp.float32
    )


def tiles_kernel(place_ref, *refs):
    ins, (out_ref, left_all, right_all, dots) = refs[:-4], refs[-4:]
    rows = ins[0].shape[0]
    share = rows // SIZES["x"]
    zl, core = place_ref[0], place_ref[1]
    at = 0
    for ref in ins[:4]:
        left_all[at : at + ref.shape[0]] = ref[...]
        at += ref.shape[0]
    at = 0
    for ref in ins[4:]:
        right_all[at : at + ref.shape[0]] = ref[...]
        at += ref.shape[0]
    dots[...] = product(left_all[...], right_all[...])
    own = dots[:rows, :rows]
    high = own.astype(jnp.bfloat16)
    low = (own - high.astype(jnp.float32)).astype(jnp.bfloat16)
    for x in range(SIZES["x"]):
        out_ref[x, 4 * EACH] = high[x * share : (x + 1) * share]
        out_ref[x, 4 * EACH + 1] = low[x * share : (x + 1) * share]
    for flip in range(4):
        target = jnp.bitwise_xor(zl, flip)
        for other in range(2):
            side = jnp.bitwise_xor(core, other)
            first = jnp.where(zl * 2 + side > target * 2 + core, 0, 1)
            for t in range(FAR):
                start = pl.multiple_of((other * (FAR + 1) + t + first) * rows, rows)
                tile = dots[flip * rows : (flip + 1) * rows, pl.ds(start, rows)]
                tile = tile.astype(jnp.bfloat16)
                for x in range(SIZES["x"]):
                    out_ref[x, target * EACH + side * FAR + t] = tile[
                        x * share : (x + 1) * share
                    ]


def first_sum_kernel(parts_ref, out_ref):
    half = out_ref.shape[2]

    def total(tile):
        acc = parts_ref[0, tile].astype(jnp.float32)
        for x in range(1, SIZES["x"]):
            acc = acc + parts_ref[x, tile].astype(jnp.float32)
        return acc

    own = total(4 * EACH) + total(4 * EACH + 1)
    high = own.astype(jnp.bfloat16)
    low = (own - high.astype(jnp.float32)).astype(jnp.bfloat16)
    for target in range(4):
        for n in range(EACH + 2):
            if n < EACH:
                tile = total(target * EACH + n).astype(jnp.bfloat16)
            else:
                tile = high if n == EACH else low
            for h in range(SIZES["zh"]):
                out_ref[target * SIZES["zh"] + h, n] = tile[h * half : (h + 1) * half]


def last_sum_kernel(factor, place_ref, parts_ref, out_ref):
    mine = place_ref[0] * 2 + place_ref[1]
    own = jnp.zeros(out_ref.shape[2:], jnp.float32)
    for h in range(SIZES["zh"]):
        for n in (EACH, EACH + 1):
            own = own + parts_ref[place_ref[0] * 2 + h, n].astype(jnp.float32)
    out_ref[0, 0] = own * factor
    for j in range(1, ROW + 1):
        source = lax.rem(mine + j, ROW)
        zl, core = lax.div(source, 2), lax.rem(source, 2)
        for t in range(FAR):
            a = parts_ref[zl * 2, core * FAR + t].astype(jnp.float32)
            b = parts_ref[zl * 2 + 1, core * FAR + t].astype(jnp.float32)
            out_ref[0, ROW * t + j] = (a + b) * factor


def on_device(snapshots, counts, weights):
    rows, points = snapshots.shape
    slot_index = lax.broadcasted_iota(jnp.int32, (rows, 1), 0)
    masked = jnp.where(slot_index < counts[0], snapshots, jnp.zeros_like(snapshots))
    weighted = (masked.astype(jnp.float32) * weights[None, :]).astype(jnp.bfloat16)
    place = jnp.stack([lax.axis_index("zl"), lax.axis_index("core")]).astype(jnp.int32)

    z2, z1 = across(weighted, 2), across(weighted, 1)
    z3 = across(z2, 1)
    r4, r1 = ahead(masked, 4), ahead(masked, 1)
    r3, r2 = ahead(r4, -1), ahead(r1, 1)
    lefts = [weighted, z1, z2, z3]
    rights = [masked, r1, r2, r3, r4]
    rights = rights + [swapped(b) for b in rights]

    share, half = rows // SIZES["x"], rows // (SIZES["x"] * SIZES["zh"])
    tiles = pl.pallas_call(
        tiles_kernel,
        out_shape=jax.ShapeDtypeStruct((SIZES["x"], 4 * EACH + 2, share, rows), jnp.bfloat16),
        in_specs=[SMEM] + [VMEM] * 14,
        out_specs=VMEM,
        scratch_shapes=[
            pltpu.VMEM((4 * rows, points), jnp.bfloat16),
            pltpu.VMEM((10 * rows, points), jnp.bfloat16),
            pltpu.VMEM((4 * rows, 10 * rows), jnp.float32),
        ],
        compiler_params=PARAMS,
    )(place, *lefts, *rights)
    parts = lax.all_to_all(tiles, "x", 0, 0, tiled=True)
    sums = pl.pallas_call(
        first_sum_kernel,
        out_shape=jax.ShapeDtypeStruct((4 * SIZES["zh"], EACH + 2, half, rows), jnp.bfloat16),
        in_specs=[VMEM],
        out_specs=VMEM,
        compiler_params=PARAMS,
    )(parts)
    shares = lax.all_to_all(sums, ("zl", "zh"), 0, 0, tiled=True)
    factor = 1.0 / math.sqrt(points * SIZES["x"] * SIZES["zh"])
    return pl.pallas_call(
        functools.partial(last_sum_kernel, factor),
        out_shape=jax.ShapeDtypeStruct((1, ROW * FAR + 1, half, rows), jnp.float32),
        in_specs=[SMEM, VMEM],
        out_specs=VMEM,
        compiler_params=PARAMS,
    )(place, shares)


def solution(mesh):
    fine = Mesh(mesh.devices.reshape(tuple(SIZES.values())), tuple(SIZES))
    snap, space = ("y", "zl", "core"), ("x", "zh")
    return jax.shard_map(
        on_device,
        mesh=fine,
        in_specs=(P(snap, space), P(snap), P(space)),
        out_specs=P(snap, None, space, None),
        check_vma=False,
    )
```

```python
import functools
import math

import jax
import jax.numpy as jnp
from jax import lax
from jax.experimental import pallas as pl
from jax.experimental.pallas import tpu as pltpu
from jax.sharding import Mesh
from jax.sharding import PartitionSpec as P

SIZES = {"y": 8, "zl": 4, "core": 2, "x": 4, "zh": 2}
ROW = 8
FAR = 4
EACH = 8
VMEM = pl.BlockSpec(memory_space=pltpu.VMEM)
SMEM = pl.BlockSpec(memory_space=pltpu.SMEM)
PARAMS = pltpu.CompilerParams(vmem_limit_bytes=32 * 1024 * 1024)


def ahead(block, by):
    return lax.ppermute(block, "y", [(i, (i - by) % SIZES["y"]) for i in range(SIZES["y"])])


def across(block, flip):
    return lax.ppermute(block, "zl", [(i, i ^ flip) for i in range(SIZES["zl"])])


def swapped(block):
    return lax.ppermute(block, "core", [(0, 1), (1, 0)])


def product(left_rows, right_rows):
    return lax.dot_general(
        left_rows, right_rows, (((1,), (1,)), ((), ())), preferred_element_type=jnp.float32
    )


def tiles_kernel(place_ref, *refs):
    ins, (out_ref, left_all, right_all, dots) = refs[:-4], refs[-4:]
    rows = ins[0].shape[0]
    share = rows // SIZES["x"]
    zl, core = place_ref[0], place_ref[1]
    at = 0
    for ref in ins[:4]:
        left_all[at : at + ref.shape[0]] = ref[...]
        at += ref.shape[0]
    at = 0
    for ref in ins[4:]:
        right_all[at : at + ref.shape[0]] = ref[...]
        at += ref.shape[0]
    dots[...] = product(left_all[...], right_all[...])
    own = dots[:rows, :rows]
    high = own.astype(jnp.bfloat16)
    low = (own - high.astype(jnp.float32)).astype(jnp.bfloat16)
    for x in range(SIZES["x"]):
        out_ref[x, 4 * EACH] = high[x * share : (x + 1) * share]
        out_ref[x, 4 * EACH + 1] = low[x * share : (x + 1) * share]
    for flip in range(4):
        target = jnp.bitwise_xor(zl, flip)
        for other in range(2):
            side = jnp.bitwise_xor(core, other)
            first = jnp.where(zl * 2 + side > target * 2 + core, 0, 1)
            for t in range(FAR):
                start = pl.multiple_of((other * (FAR + 1) + t + first) * rows, rows)
                tile = dots[flip * rows : (flip + 1) * rows, pl.ds(start, rows)]
                tile = tile.astype(jnp.bfloat16)
                for x in range(SIZES["x"]):
                    out_ref[x, target * EACH + side * FAR + t] = tile[
                        x * share : (x + 1) * share
                    ]


def first_sum_kernel(parts_ref, out_ref):
    half = out_ref.shape[2]

    def total(tile):
        acc = parts_ref[0, tile].astype(jnp.float32)
        for x in range(1, SIZES["x"]):
            acc = acc + parts_ref[x, tile].astype(jnp.float32)
        return acc

    own = total(4 * EACH) + total(4 * EACH + 1)
    high = own.astype(jnp.bfloat16)
    low = (own - high.astype(jnp.float32)).astype(jnp.bfloat16)
    for target in range(4):
        for n in range(EACH + 2):
            if n < EACH:
                tile = total(target * EACH + n).astype(jnp.bfloat16)
            else:
                tile = high if n == EACH else low
            for h in range(SIZES["zh"]):
                out_ref[target * SIZES["zh"] + h, n] = tile[h * half : (h + 1) * half]


def last_sum_kernel(factor, place_ref, parts_ref, out_ref):
    mine = place_ref[0] * 2 + place_ref[1]
    own = jnp.zeros(out_ref.shape[2:], jnp.float32)
    for h in range(SIZES["zh"]):
        for n in (EACH, EACH + 1):
            own = own + parts_ref[place_ref[0] * 2 + h, n].astype(jnp.float32)
    out_ref[0, 0] = own * factor
    for j in range(1, ROW + 1):
        source = lax.rem(mine + j, ROW)
        zl, core = lax.div(source, 2), lax.rem(source, 2)
        for t in range(FAR):
            a = parts_ref[zl * 2, core * FAR + t].astype(jnp.float32)
            b = parts_ref[zl * 2 + 1, core * FAR + t].astype(jnp.float32)
            out_ref[0, ROW * t + j] = (a + b) * factor


def on_device(snapshots, counts, weights):
    rows, points = snapshots.shape
    slot_index = lax.broadcasted_iota(jnp.int32, (rows, 1), 0)
    masked = jnp.where(slot_index < counts[0], snapshots, jnp.zeros_like(snapshots))
    weighted = (masked.astype(jnp.float32) * weights[None, :]).astype(jnp.bfloat16)
    place = jnp.stack([lax.axis_index("zl"), lax.axis_index("core")]).astype(jnp.int32)

    tie = lax.optimization_barrier
    r1, r4 = ahead(masked, 1), ahead(masked, 4)
    z2, z1 = across(weighted, 2), across(weighted, 1)
    r2, r3 = ahead(r1, 1), ahead(r4, -1)
    r4, z2 = tie((r4, z2))
    z3 = across(z2, 1)
    pair = jnp.concatenate([masked, r1])
    lefts = [weighted, z1, z2, z3]
    rights = [pair, r2, r3, r4, swapped(pair), swapped(r2), swapped(r3), swapped(r4)]

    share, half = rows // SIZES["x"], rows // (SIZES["x"] * SIZES["zh"])
    tiles = pl.pallas_call(
        tiles_kernel,
        out_shape=jax.ShapeDtypeStruct((SIZES["x"], 4 * EACH + 2, share, rows), jnp.bfloat16),
        in_specs=[SMEM] + [VMEM] * 12,
        out_specs=VMEM,
        scratch_shapes=[
            pltpu.VMEM((4 * rows, points), jnp.bfloat16),
            pltpu.VMEM((10 * rows, points), jnp.bfloat16),
            pltpu.VMEM((4 * rows, 10 * rows), jnp.float32),
        ],
        compiler_params=PARAMS,
    )(place, *lefts, *rights)
    parts = lax.all_to_all(tiles, "x", 0, 0, tiled=True)
    sums = pl.pallas_call(
        first_sum_kernel,
        out_shape=jax.ShapeDtypeStruct((4 * SIZES["zh"], EACH + 2, half, rows), jnp.bfloat16),
        in_specs=[VMEM],
        out_specs=VMEM,
        compiler_params=PARAMS,
    )(parts)
    shares = lax.all_to_all(sums, ("zl", "zh"), 0, 0, tiled=True)
    factor = 1.0 / math.sqrt(points * SIZES["x"] * SIZES["zh"])
    return pl.pallas_call(
        functools.partial(last_sum_kernel, factor),
        out_shape=jax.ShapeDtypeStruct((1, ROW * FAR + 1, half, rows), jnp.float32),
        in_specs=[SMEM, VMEM],
        out_specs=VMEM,
        compiler_params=PARAMS,
    )(place, shares)


def solution(mesh):
    fine = Mesh(mesh.devices.reshape(tuple(SIZES.values())), tuple(SIZES))
    snap, space = ("y", "zl", "core"), ("x", "zh")
    return jax.shard_map(
        on_device,
        mesh=fine,
        in_specs=(P(snap, space), P(snap), P(space)),
        out_specs=P(snap, None, space, None),
        check_vma=False,
    )
```

```python
import functools
import math

import jax
import jax.numpy as jnp
from jax import lax
from jax.experimental import pallas as pl
from jax.experimental.pallas import tpu as pltpu
from jax.sharding import Mesh
from jax.sharding import PartitionSpec as P

SIZES = {"y": 8, "zl": 4, "core": 2, "x": 4, "zh": 2}
ROW = 8
FAR = 4
EACH = 8
VMEM = pl.BlockSpec(memory_space=pltpu.VMEM)
SMEM = pl.BlockSpec(memory_space=pltpu.SMEM)
PARAMS = pltpu.CompilerParams(vmem_limit_bytes=32 * 1024 * 1024)


def ahead(block, by):
    return lax.ppermute(block, "y", [(i, (i - by) % SIZES["y"]) for i in range(SIZES["y"])])


def across(block, flip):
    return lax.ppermute(block, "zl", [(i, i ^ flip) for i in range(SIZES["zl"])])


def swapped(block):
    return lax.ppermute(block, "core", [(0, 1), (1, 0)])


def product(left_rows, right_rows):
    return lax.dot_general(
        left_rows, right_rows, (((1,), (1,)), ((), ())), preferred_element_type=jnp.float32
    )


def tiles_kernel(place_ref, *refs):
    ins, (out_ref, left_all, right_all, dots) = refs[:-4], refs[-4:]
    rows = ins[0].shape[0]
    share = rows // SIZES["x"]
    zl, core = place_ref[0], place_ref[1]
    at = 0
    for ref in ins[:4]:
        left_all[at : at + ref.shape[0]] = ref[...]
        at += ref.shape[0]
    at = 0
    for ref in ins[4:]:
        right_all[at : at + ref.shape[0]] = ref[...]
        at += ref.shape[0]
    dots[...] = product(left_all[...], right_all[...])
    own = dots[:rows, :rows]
    high = own.astype(jnp.bfloat16)
    low = (own - high.astype(jnp.float32)).astype(jnp.bfloat16)
    for x in range(SIZES["x"]):
        out_ref[x, 4 * EACH] = high[x * share : (x + 1) * share]
        out_ref[x, 4 * EACH + 1] = low[x * share : (x + 1) * share]
    for flip in range(4):
        target = jnp.bitwise_xor(zl, flip)
        for other in range(2):
            side = jnp.bitwise_xor(core, other)
            first = jnp.where(zl * 2 + side > target * 2 + core, 0, 1)
            for t in range(FAR):
                start = pl.multiple_of((other * (FAR + 1) + t + first) * rows, rows)
                tile = dots[flip * rows : (flip + 1) * rows, pl.ds(start, rows)]
                tile = tile.astype(jnp.bfloat16)
                for x in range(SIZES["x"]):
                    out_ref[x, target * EACH + side * FAR + t] = tile[
                        x * share : (x + 1) * share
                    ]


def first_sum_kernel(parts_ref, out_ref):
    half = out_ref.shape[2]

    def total(tile):
        acc = parts_ref[0, tile].astype(jnp.float32)
        for x in range(1, SIZES["x"]):
            acc = acc + parts_ref[x, tile].astype(jnp.float32)
        return acc

    own = total(4 * EACH) + total(4 * EACH + 1)
    high = own.astype(jnp.bfloat16)
    low = (own - high.astype(jnp.float32)).astype(jnp.bfloat16)
    for target in range(4):
        for n in range(EACH + 2):
            if n < EACH:
                tile = total(target * EACH + n).astype(jnp.bfloat16)
            else:
                tile = high if n == EACH else low
            for h in range(SIZES["zh"]):
                out_ref[target * SIZES["zh"] + h, n] = tile[h * half : (h + 1) * half]


def last_sum_kernel(factor, place_ref, parts_ref, out_ref):
    mine = place_ref[0] * 2 + place_ref[1]
    own = jnp.zeros(out_ref.shape[2:], jnp.float32)
    for h in range(SIZES["zh"]):
        for n in (EACH, EACH + 1):
            own = own + parts_ref[place_ref[0] * 2 + h, n].astype(jnp.float32)
    out_ref[0, 0] = own * factor
    for j in range(1, ROW + 1):
        source = lax.rem(mine + j, ROW)
        zl, core = lax.div(source, 2), lax.rem(source, 2)
        for t in range(FAR):
            a = parts_ref[zl * 2, core * FAR + t].astype(jnp.float32)
            b = parts_ref[zl * 2 + 1, core * FAR + t].astype(jnp.float32)
            out_ref[0, ROW * t + j] = (a + b) * factor


def on_device(snapshots, counts, weights):
    rows, points = snapshots.shape
    slot_index = lax.broadcasted_iota(jnp.int32, (rows, 1), 0)
    masked = jnp.where(slot_index < counts[0], snapshots, jnp.zeros_like(snapshots))
    weighted = (masked.astype(jnp.float32) * weights[None, :]).astype(jnp.bfloat16)
    place = jnp.stack([lax.axis_index("zl"), lax.axis_index("core")]).astype(jnp.int32)

    tie = lax.optimization_barrier
    r1, r4 = ahead(masked, 1), ahead(masked, 4)
    z2, z1 = across(weighted, 2), across(weighted, 1)
    r2 = ahead(r1, 1)
    r4t, z1 = tie((r4, z1))
    r3 = ahead(r4, -1)
    r1t, z2 = tie((r1, z2))
    z3 = across(z2, 1)
    lefts = [weighted, z1, z2, z3]
    rights = [masked, r1, r2, r3, r4]
    rights = rights + [swapped(b) for b in (masked, r1t, r2, r3, r4t)]

    share, half = rows // SIZES["x"], rows // (SIZES["x"] * SIZES["zh"])
    tiles = pl.pallas_call(
        tiles_kernel,
        out_shape=jax.ShapeDtypeStruct((SIZES["x"], 4 * EACH + 2, share, rows), jnp.bfloat16),
        in_specs=[SMEM] + [VMEM] * 14,
        out_specs=VMEM,
        scratch_shapes=[
            pltpu.VMEM((4 * rows, points), jnp.bfloat16),
            pltpu.VMEM((10 * rows, points), jnp.bfloat16),
            pltpu.VMEM((4 * rows, 10 * rows), jnp.float32),
        ],
        compiler_params=PARAMS,
    )(place, *lefts, *rights)
    parts = lax.all_to_all(tiles, "x", 0, 0, tiled=True)
    sums = pl.pallas_call(
        first_sum_kernel,
        out_shape=jax.ShapeDtypeStruct((4 * SIZES["zh"], EACH + 2, half, rows), jnp.bfloat16),
        in_specs=[VMEM],
        out_specs=VMEM,
        compiler_params=PARAMS,
    )(parts)
    shares = lax.all_to_all(sums, ("zl", "zh"), 0, 0, tiled=True)
    factor = 1.0 / math.sqrt(points * SIZES["x"] * SIZES["zh"])
    return pl.pallas_call(
        functools.partial(last_sum_kernel, factor),
        out_shape=jax.ShapeDtypeStruct((1, ROW * FAR + 1, half, rows), jnp.float32),
        in_specs=[SMEM, VMEM],
        out_specs=VMEM,
        compiler_params=PARAMS,
    )(place, shares)


def solution(mesh):
    fine = Mesh(mesh.devices.reshape(tuple(SIZES.values())), tuple(SIZES))
    snap, space = ("y", "zl", "core"), ("x", "zh")
    return jax.shard_map(
        on_device,
        mesh=fine,
        in_specs=(P(snap, space), P(snap), P(space)),
        out_specs=P(snap, None, space, None),
        check_vma=False,
    )
```

```python
import functools
import math

import jax
import jax.numpy as jnp
from jax import lax
from jax.experimental import pallas as pl
from jax.experimental.pallas import tpu as pltpu
from jax.sharding import Mesh
from jax.sharding import PartitionSpec as P

SIZES = {"y": 8, "zl": 4, "core": 2, "x": 4, "zh": 2}
ROW = 8
FAR = 4
EACH = 8
VMEM = pl.BlockSpec(memory_space=pltpu.VMEM)
SMEM = pl.BlockSpec(memory_space=pltpu.SMEM)
PARAMS = pltpu.CompilerParams(vmem_limit_bytes=32 * 1024 * 1024)


def ahead(block, by):
    return lax.ppermute(block, "y", [(i, (i - by) % SIZES["y"]) for i in range(SIZES["y"])])


def across(block, flip):
    return lax.ppermute(block, "zl", [(i, i ^ flip) for i in range(SIZES["zl"])])


def swapped(block):
    return lax.ppermute(block, "core", [(0, 1), (1, 0)])


def product(left_rows, right_rows):
    return lax.dot_general(
        left_rows, right_rows, (((1,), (1,)), ((), ())), preferred_element_type=jnp.float32
    )


def tiles_kernel(place_ref, *refs):
    ins, (out_ref, left_all, right_all, dots) = refs[:-4], refs[-4:]
    rows = ins[0].shape[0]
    share = rows // SIZES["x"]
    zl, core = place_ref[0], place_ref[1]
    at = 0
    for ref in ins[:4]:
        left_all[at : at + ref.shape[0]] = ref[...]
        at += ref.shape[0]
    at = 0
    for ref in ins[4:]:
        right_all[at : at + ref.shape[0]] = ref[...]
        at += ref.shape[0]
    dots[...] = product(left_all[...], right_all[...])
    own = dots[:rows, :rows]
    high = own.astype(jnp.bfloat16)
    low = (own - high.astype(jnp.float32)).astype(jnp.bfloat16)
    for x in range(SIZES["x"]):
        out_ref[x, 4 * EACH] = high[x * share : (x + 1) * share]
        out_ref[x, 4 * EACH + 1] = low[x * share : (x + 1) * share]
    for flip in range(4):
        target = jnp.bitwise_xor(zl, flip)
        for other in range(2):
            side = jnp.bitwise_xor(core, other)
            first = jnp.where(zl * 2 + side > target * 2 + core, 0, 1)
            for t in range(FAR):
                start = pl.multiple_of((other * (FAR + 1) + t + first) * rows, rows)
                tile = dots[flip * rows : (flip + 1) * rows, pl.ds(start, rows)]
                tile = tile.astype(jnp.bfloat16)
                for x in range(SIZES["x"]):
                    out_ref[x, target * EACH + side * FAR + t] = tile[
                        x * share : (x + 1) * share
                    ]


def first_sum_kernel(parts_ref, out_ref):
    half = out_ref.shape[2]

    def total(tile):
        acc = parts_ref[0, tile].astype(jnp.float32)
        for x in range(1, SIZES["x"]):
            acc = acc + parts_ref[x, tile].astype(jnp.float32)
        return acc

    own = total(4 * EACH) + total(4 * EACH + 1)
    high = own.astype(jnp.bfloat16)
    low = (own - high.astype(jnp.float32)).astype(jnp.bfloat16)
    for target in range(4):
        for n in range(EACH + 2):
            if n < EACH:
                tile = total(target * EACH + n).astype(jnp.bfloat16)
            else:
                tile = high if n == EACH else low
            for h in range(SIZES["zh"]):
                out_ref[target * SIZES["zh"] + h, n] = tile[h * half : (h + 1) * half]


def last_sum_kernel(factor, place_ref, parts_ref, out_ref):
    mine = place_ref[0] * 2 + place_ref[1]
    own = jnp.zeros(out_ref.shape[2:], jnp.float32)
    for h in range(SIZES["zh"]):
        for n in (EACH, EACH + 1):
            own = own + parts_ref[place_ref[0] * 2 + h, n].astype(jnp.float32)
    out_ref[0, 0] = own * factor
    for j in range(1, ROW + 1):
        source = lax.rem(mine + j, ROW)
        zl, core = lax.div(source, 2), lax.rem(source, 2)
        for t in range(FAR):
            a = parts_ref[zl * 2, core * FAR + t].astype(jnp.float32)
            b = parts_ref[zl * 2 + 1, core * FAR + t].astype(jnp.float32)
            out_ref[0, ROW * t + j] = (a + b) * factor


def on_device(snapshots, counts, weights):
    rows, points = snapshots.shape
    slot_index = lax.broadcasted_iota(jnp.int32, (rows, 1), 0)
    masked = jnp.where(slot_index < counts[0], snapshots, jnp.zeros_like(snapshots))
    weighted = (masked.astype(jnp.float32) * weights[None, :]).astype(jnp.bfloat16)
    place = jnp.stack([lax.axis_index("zl"), lax.axis_index("core")]).astype(jnp.int32)

    tie = lax.optimization_barrier
    r1, r4 = ahead(masked, 1), ahead(masked, 4)
    z2, z1 = across(weighted, 2), across(weighted, 1)
    r2 = ahead(r1, 1)
    r1t, z1 = tie((r1, z1))
    r3 = ahead(r4, -1)
    r4t, z2 = tie((r4, z2))
    z3 = across(z2, 1)
    lefts = [weighted, z1, z2, z3]
    rights = [masked, r1, r2, r3, r4]
    rights = rights + [swapped(b) for b in (masked, r1t, r2, r3, r4t)]

    share, half = rows // SIZES["x"], rows // (SIZES["x"] * SIZES["zh"])
    tiles = pl.pallas_call(
        tiles_kernel,
        out_shape=jax.ShapeDtypeStruct((SIZES["x"], 4 * EACH + 2, share, rows), jnp.bfloat16),
        in_specs=[SMEM] + [VMEM] * 14,
        out_specs=VMEM,
        scratch_shapes=[
            pltpu.VMEM((4 * rows, points), jnp.bfloat16),
            pltpu.VMEM((10 * rows, points), jnp.bfloat16),
            pltpu.VMEM((4 * rows, 10 * rows), jnp.float32),
        ],
        compiler_params=PARAMS,
    )(place, *lefts, *rights)
    parts = lax.all_to_all(tiles, "x", 0, 0, tiled=True)
    sums = pl.pallas_call(
        first_sum_kernel,
        out_shape=jax.ShapeDtypeStruct((4 * SIZES["zh"], EACH + 2, half, rows), jnp.bfloat16),
        in_specs=[VMEM],
        out_specs=VMEM,
        compiler_params=PARAMS,
    )(parts)
    shares = lax.all_to_all(sums, ("zl", "zh"), 0, 0, tiled=True)
    factor = 1.0 / math.sqrt(points * SIZES["x"] * SIZES["zh"])
    return pl.pallas_call(
        functools.partial(last_sum_kernel, factor),
        out_shape=jax.ShapeDtypeStruct((1, ROW * FAR + 1, half, rows), jnp.float32),
        in_specs=[SMEM, VMEM],
        out_specs=VMEM,
        compiler_params=PARAMS,
    )(place, shares)


def solution(mesh):
    fine = Mesh(mesh.devices.reshape(tuple(SIZES.values())), tuple(SIZES))
    snap, space = ("y", "zl", "core"), ("x", "zh")
    return jax.shard_map(
        on_device,
        mesh=fine,
        in_specs=(P(snap, space), P(snap), P(space)),
        out_specs=P(snap, None, space, None),
        check_vma=False,
    )
```

```python
import functools
import math

import jax
import jax.numpy as jnp
from jax import lax
from jax.experimental import pallas as pl
from jax.experimental.pallas import tpu as pltpu
from jax.sharding import Mesh
from jax.sharding import PartitionSpec as P

SIZES = {"y": 8, "zl": 4, "core": 2, "x": 4, "zh": 2}
ROW = 8
FAR = 4
EACH = 8
VMEM = pl.BlockSpec(memory_space=pltpu.VMEM)
SMEM = pl.BlockSpec(memory_space=pltpu.SMEM)
PARAMS = pltpu.CompilerParams(vmem_limit_bytes=32 * 1024 * 1024)


def ahead(block, by):
    return lax.ppermute(block, "y", [(i, (i - by) % SIZES["y"]) for i in range(SIZES["y"])])


def across(block, flip):
    return lax.ppermute(block, "zl", [(i, i ^ flip) for i in range(SIZES["zl"])])


def swapped(block):
    return lax.ppermute(block, "core", [(0, 1), (1, 0)])


def product(left_rows, right_rows):
    return lax.dot_general(
        left_rows, right_rows, (((1,), (1,)), ((), ())), preferred_element_type=jnp.float32
    )


def tiles_kernel(place_ref, *refs):
    ins, (out_ref, left_all, right_all, dots) = refs[:-4], refs[-4:]
    rows = ins[0].shape[0]
    share = rows // SIZES["x"]
    zl, core = place_ref[0], place_ref[1]
    at = 0
    for ref in ins[:4]:
        left_all[at : at + ref.shape[0]] = ref[...]
        at += ref.shape[0]
    at = 0
    for ref in ins[4:]:
        right_all[at : at + ref.shape[0]] = ref[...]
        at += ref.shape[0]
    half = (FAR + 1) * rows
    dots[:, :half] = product(left_all[...], right_all[:half])
    dots[:, half:] = product(left_all[...], right_all[half:])
    own = dots[:rows, :rows]
    high = own.astype(jnp.bfloat16)
    low = (own - high.astype(jnp.float32)).astype(jnp.bfloat16)
    for x in range(SIZES["x"]):
        out_ref[x, 4 * EACH] = high[x * share : (x + 1) * share]
        out_ref[x, 4 * EACH + 1] = low[x * share : (x + 1) * share]
    for flip in range(4):
        target = jnp.bitwise_xor(zl, flip)
        for other in range(2):
            side = jnp.bitwise_xor(core, other)
            first = jnp.where(zl * 2 + side > target * 2 + core, 0, 1)
            for t in range(FAR):
                start = pl.multiple_of((other * (FAR + 1) + t + first) * rows, rows)
                tile = dots[flip * rows : (flip + 1) * rows, pl.ds(start, rows)]
                tile = tile.astype(jnp.bfloat16)
                for x in range(SIZES["x"]):
                    out_ref[x, target * EACH + side * FAR + t] = tile[
                        x * share : (x + 1) * share
                    ]


def first_sum_kernel(parts_ref, out_ref):
    half = out_ref.shape[2]

    def total(tile):
        acc = parts_ref[0, tile].astype(jnp.float32)
        for x in range(1, SIZES["x"]):
            acc = acc + parts_ref[x, tile].astype(jnp.float32)
        return acc

    own = total(4 * EACH) + total(4 * EACH + 1)
    high = own.astype(jnp.bfloat16)
    low = (own - high.astype(jnp.float32)).astype(jnp.bfloat16)
    for target in range(4):
        for n in range(EACH + 2):
            if n < EACH:
                tile = total(target * EACH + n).astype(jnp.bfloat16)
            else:
                tile = high if n == EACH else low
            for h in range(SIZES["zh"]):
                out_ref[target * SIZES["zh"] + h, n] = tile[h * half : (h + 1) * half]


def last_sum_kernel(factor, place_ref, parts_ref, out_ref):
    mine = place_ref[0] * 2 + place_ref[1]
    own = jnp.zeros(out_ref.shape[2:], jnp.float32)
    for h in range(SIZES["zh"]):
        for n in (EACH, EACH + 1):
            own = own + parts_ref[place_ref[0] * 2 + h, n].astype(jnp.float32)
    out_ref[0, 0] = own * factor
    for j in range(1, ROW + 1):
        source = lax.rem(mine + j, ROW)
        zl, core = lax.div(source, 2), lax.rem(source, 2)
        for t in range(FAR):
            a = parts_ref[zl * 2, core * FAR + t].astype(jnp.float32)
            b = parts_ref[zl * 2 + 1, core * FAR + t].astype(jnp.float32)
            out_ref[0, ROW * t + j] = (a + b) * factor


def on_device(snapshots, counts, weights):
    rows, points = snapshots.shape
    slot_index = lax.broadcasted_iota(jnp.int32, (rows, 1), 0)
    masked = jnp.where(slot_index < counts[0], snapshots, jnp.zeros_like(snapshots))
    weighted = (masked.astype(jnp.float32) * weights[None, :]).astype(jnp.bfloat16)
    place = jnp.stack([lax.axis_index("zl"), lax.axis_index("core")]).astype(jnp.int32)

    tie = lax.optimization_barrier
    r1, r4 = ahead(masked, 1), ahead(masked, 4)
    z2, z1 = across(weighted, 2), across(weighted, 1)
    r2 = ahead(r1, 1)
    r4t, z1 = tie((r4, z1))
    r3 = ahead(r4, -1)
    r1t, z2 = tie((r1, z2))
    z3 = across(z2, 1)
    lefts = [weighted, z1, z2, z3]
    rights = [masked, r1, r2, r3, r4]
    rights = rights + [swapped(b) for b in (masked, r1t, r2, r3, r4t)]

    share, half = rows // SIZES["x"], rows // (SIZES["x"] * SIZES["zh"])
    tiles = pl.pallas_call(
        tiles_kernel,
        out_shape=jax.ShapeDtypeStruct((SIZES["x"], 4 * EACH + 2, share, rows), jnp.bfloat16),
        in_specs=[SMEM] + [VMEM] * 14,
        out_specs=VMEM,
        scratch_shapes=[
            pltpu.VMEM((4 * rows, points), jnp.bfloat16),
            pltpu.VMEM((10 * rows, points), jnp.bfloat16),
            pltpu.VMEM((4 * rows, 10 * rows), jnp.float32),
        ],
        compiler_params=PARAMS,
    )(place, *lefts, *rights)
    parts = lax.all_to_all(tiles, "x", 0, 0, tiled=True)
    sums = pl.pallas_call(
        first_sum_kernel,
        out_shape=jax.ShapeDtypeStruct((4 * SIZES["zh"], EACH + 2, half, rows), jnp.bfloat16),
        in_specs=[VMEM],
        out_specs=VMEM,
        compiler_params=PARAMS,
    )(parts)
    shares = lax.all_to_all(sums, ("zl", "zh"), 0, 0, tiled=True)
    factor = 1.0 / math.sqrt(points * SIZES["x"] * SIZES["zh"])
    return pl.pallas_call(
        functools.partial(last_sum_kernel, factor),
        out_shape=jax.ShapeDtypeStruct((1, ROW * FAR + 1, half, rows), jnp.float32),
        in_specs=[SMEM, VMEM],
        out_specs=VMEM,
        compiler_params=PARAMS,
    )(place, shares)


def solution(mesh):
    fine = Mesh(mesh.devices.reshape(tuple(SIZES.values())), tuple(SIZES))
    snap, space = ("y", "zl", "core"), ("x", "zh")
    return jax.shard_map(
        on_device,
        mesh=fine,
        in_specs=(P(snap, space), P(snap), P(space)),
        out_specs=P(snap, None, space, None),
        check_vma=False,
    )
```
